32 devices in a mesh: row: 8 (over y, x, core), col: 4 (over z).
Axes of the slice: x: 2, y: 2, z: 4, core: 2. Of those that a mesh axis runs over, the one named last changes fastest.
Arguments:
- frames: bfloat16 [4, 4096, 512], P(None, 'row'), may hold values from -6 to 6
- orders: int32 [2, 2], replicated, may hold values from 1 to 64
- owners: int32 [4096, 1], P(('row', 'col')), may hold values from 0 to 31; in each aligned block of 128 rows (0 to 127, 128 to 255, ...) at most 8 rows name the same one
- templates: bfloat16 [32, 512, 128], P(('row', 'col')), may hold values from -0.25 to 0.25
Outputs:
- spectrum: bfloat16 [2, 4, 4, 2048, 4096], P(None, None, None, ('row', 'col'))
- detections: bfloat16 [32, 32, 8, 64, 128], P(('row', 'col'))
The draws below stay inside these ranges and needn't reach their ends.
Inputs may be any that keep to these rules, and one draw needn't show every extreme that they name: `owners`: rows 128 * i to 128 * (i + 1) - 1 hold the tiles of the device with index i along row+col. At most 8 tiles of one device name the same owner, and some device reaches that in every draw.
All inputs are finite; a program needn't handle non-finite values.
Results may differ from the reference program's by a relative error of at most 0.0078.
Values may be sent and summed in bfloat16 or wider, within the bound.
A program may use at most 192 MiB of HBM per device.

```python
import math
import jax
import jax.numpy as jnp
import numpy as np
from jax import lax

SENSORS = 4
NCH = 2048
HOPS = 4096
RADIX = 8
WHEELS = 2
ORDERS = 2
FEAT = 128
FRAME = 512
SUB = 512
COMBOS = 4
CH_DEV = 64
TILES_DEV = 128
TILES = 4096
CAP = 8
N_ROW = 8
N_COL = 4
DEVICES = 32


def with_ends(result, key, smallest, top_value):
    place = [jax.random.randint(jax.random.fold_in(key, axis), (), 0, length) for axis, length in enumerate(result.shape)]
    main_axis = result.shape.index(max(result.shape))
    beside = place[:main_axis] + [(place[main_axis] + 1) % result.shape[main_axis]] + place[main_axis + 1:]
    return result.at[tuple(place)].set(smallest).at[tuple(beside)].set(top_value)


def level_of(rng, dims, split, low, top_value):
    def one(axis_at, parts):
        draws = jax.random.uniform(jax.random.fold_in(jax.random.fold_in(rng, 6), axis_at), (parts,), jnp.float32, low / len(split), top_value / len(split))
        return jnp.repeat(jnp.exp(draws), dims[axis_at] // parts).reshape((-1,) + (1,) * (len(dims) - axis_at - 1))

    gain = one(*split[0])
    for cut in split[1:]:
        gain = gain * one(*cut)
    return gain


def assign_block(rng, own, number, rows, number_of, top, limit, slope):
    ranking = jax.random.permutation(rng, number_of)
    heavy_load, common = load_shares(number_of, rows * top, limit, slope, True), load_shares(number_of, rows * top, limit, slope, False)
    places = jnp.arange(number_of)

    def named(lengths, rotation):
        used = int((lengths > 0).sum())
        fixed = max(1, used // 4)
        moved = fixed + (places - fixed + rotation * (used - fixed)) % max(1, number_of - fixed)
        return jnp.zeros((number_of,), jnp.int32).at[ranking[jnp.where(places < fixed, places, moved)]].set(jnp.asarray(lengths, jnp.int32))

    lengths = jnp.where(number % 4 == 0, named(heavy_load, number // 4), named(common, number - number // 4 - 1))
    mixed = jax.random.permutation(jax.random.fold_in(own, 3), number_of)
    giver, taker = mixed[0:number_of // 2 * 2:2], mixed[1:number_of // 2 * 2:2]
    room = jnp.minimum(lengths[giver] - 1, limit - lengths[taker]) // 2
    room = jnp.where((giver == ranking[0]) | (taker == ranking[0]) | (lengths[taker] == 0), 0, jnp.maximum(room, 0))
    moved = jax.random.randint(jax.random.fold_in(own, 4), (number_of // 2,), 0, 1 << 20) % (room + 1)
    lengths = lengths.at[giver].add(-moved).at[taker].add(moved)
    members = jnp.searchsorted(jnp.cumsum(lengths), jnp.arange(rows * top), side="right").astype(jnp.int32)
    listing = members.reshape(top, rows).T
    listing = listing[jax.random.permutation(jax.random.fold_in(own, 1), rows)]
    rotation = jax.random.randint(jax.random.fold_in(own, 2), (rows, 1), 0, top)
    return jnp.take_along_axis(listing, (jnp.arange(top)[None, :] + rotation) % top, axis=1)


def load_shares(amount, total, bound, lean, full):
    loads = [(1 << 20) // math.isqrt(grade ** lean) + 1 for grade in range(1, amount + 1)]
    largest = bound if full else min(bound, max(-(-total // amount), total * loads[0] // sum(loads)))
    least = 1 if total - largest >= amount - 1 else 0
    holding, surplus = [largest] + [least] * (amount - 1), total - largest - least * (amount - 1)
    while surplus > 0:
        candidates = [i for i in range(1, amount) if holding[i] < largest] or [i for i in range(1, amount) if holding[i] < bound]
        pool, remaining = sum([loads[i] for i in candidates]), surplus
        for i in candidates:
            more = min(bound - holding[i], max(1, remaining * loads[i] // pool), surplus)
            holding[i] = holding[i] + more
            surplus = surplus - more
    return np.array(holding)


def scatter_about(key, extent, width, limit, shards=(), kind=jnp.bfloat16):
    entries = width * jax.random.normal(key, extent, jnp.float32)
    if shards:
        entries = entries * level_of(key, extent, shards, -0.22, 0.18)
    return jnp.clip(entries, -limit, limit).astype(kind)


def setup_inputs(seed: int = 0) -> dict:
    keys = jax.random.split(jax.random.key(seed), 5)
    frames = scatter_about(keys[0], (SENSORS, HOPS, FRAME), 1.0, 6.0, ((1, 8),))
    orders = with_ends(jax.random.randint(keys[1], (WHEELS, ORDERS), 1, CH_DEV + 1), jax.random.fold_in(keys[1], 1), 1, CH_DEV).astype(jnp.int32)
    owners_keys = jax.random.split(jax.random.fold_in(keys[2], 1), TILES // TILES_DEV)
    owners_turns = jax.random.permutation(jax.random.fold_in(keys[2], 3), TILES // TILES_DEV)
    owners = jax.vmap(lambda own, number: assign_block(jax.random.fold_in(keys[2], 2), own, number, TILES_DEV, DEVICES, 1, CAP, 2))(owners_keys, owners_turns).reshape((TILES, 1))
    templates = scatter_about(keys[3], (DEVICES, SUB, FEAT), SUB ** -0.5, 0.25, ((0, 32),))
    return {"frames": frames, "orders": orders, "owners": owners, "templates": templates}


def channel_coefficients(n_total, channel_ids):
    position = jnp.arange(n_total, dtype=jnp.int32)
    turns = position[:, None] * channel_ids[None, :] % n_total
    phase_angle = 2.0 * math.pi / n_total * turns.astype(jnp.float32)
    window = 0.5 - 0.5 * jnp.cos(2.0 * math.pi / n_total * position.astype(jnp.float32))
    gain_factor = math.sqrt(8.0 / (3.0 * n_total))
    weighted = gain_factor * window[:, None]
    both = jnp.concatenate([weighted * jnp.cos(phase_angle), weighted * jnp.sin(phase_angle)], axis=1)
    return both.astype(jnp.bfloat16)

def sub_coefficients(sub_total):
    index_a = jnp.arange(sub_total, dtype=jnp.int32)
    turns = index_a[:, None] * index_a[None, :] % sub_total
    phase_angle = 2.0 * math.pi / sub_total * turns.astype(jnp.float32)
    return jnp.concatenate([jnp.cos(phase_angle), jnp.sin(phase_angle)], axis=1).astype(jnp.bfloat16)

def quarter_turn(a_cos, a_sin, channel_ids, hop_ids):
    phase_step = channel_ids[:, None] % 4 * (hop_ids[None, :] % 4) % 4
    cos_quarter = (phase_step == 0).astype(jnp.float32) - (phase_step == 2).astype(jnp.float32)
    sin_quarter = (phase_step == 1).astype(jnp.float32) - (phase_step == 3).astype(jnp.float32)
    real_part = a_cos * cos_quarter - a_sin * sin_quarter
    imag_part = -a_sin * cos_quarter - a_cos * sin_quarter
    return (real_part, imag_part)

def finish_transform(first_real, first_imag, hops_total):
    radix_count = first_real.shape[-2]
    sub_total = first_real.shape[-1]
    index_b = jnp.arange(radix_count, dtype=jnp.int32)[:, None]
    index_p = jnp.arange(sub_total, dtype=jnp.int32)[None, :]
    twist_angle = 2.0 * math.pi / hops_total * (index_b * index_p % hops_total).astype(jnp.float32)
    twist_cos = jnp.cos(twist_angle)
    twist_sin = jnp.sin(twist_angle)
    twist_real = first_real * twist_cos + first_imag * twist_sin
    twist_imag = first_imag * twist_cos - first_real * twist_sin
    index_d = jnp.arange(radix_count, dtype=jnp.int32)[None, :]
    section_angle = 2.0 * math.pi / radix_count * (index_b * index_d % radix_count).astype(jnp.float32)
    section_cos = jnp.cos(section_angle)
    section_sin = jnp.sin(section_angle)
    highest = lax.Precision.HIGHEST
    norm_factor = 1.0 / math.sqrt(hops_total)
    out_real = norm_factor * (jnp.einsum('...bq,bd->...dq', twist_real, section_cos, precision=highest) + jnp.einsum('...bq,bd->...dq', twist_imag, section_sin, precision=highest))
    out_imag = norm_factor * (jnp.einsum('...bq,bd->...dq', twist_imag, section_cos, precision=highest) - jnp.einsum('...bq,bd->...dq', twist_real, section_sin, precision=highest))
    return (out_real, out_imag)

def reference(frames, orders, owners, templates):
    devices_n = N_ROW * N_COL
    every_channel = jnp.arange(NCH, dtype=jnp.int32)
    coefficients = channel_coefficients(NCH, every_channel)
    table_sub = sub_coefficients(SUB)
    cos_sub = table_sub[:, :SUB].astype(jnp.float32)
    sin_sub = table_sub[:, SUB:].astype(jnp.float32)
    hop_ids = jnp.arange(HOPS, dtype=jnp.int32)
    spectra = []
    features = []
    for sensor in range(SENSORS):
        padded = jnp.concatenate([frames[sensor], jnp.zeros((3, FRAME), frames.dtype)], axis=0)
        summed = jnp.zeros((2 * NCH, HOPS), jnp.float32)
        for quarter in range(4):
            summed = summed + jnp.einsum('hf,fk->kh', padded[quarter:quarter + HOPS].astype(jnp.float32), coefficients[quarter * FRAME:(quarter + 1) * FRAME].astype(jnp.float32))
        real_part, imag_part = quarter_turn(summed[:NCH], summed[NCH:], every_channel, hop_ids)
        demod = jnp.stack([real_part, imag_part]).astype(jnp.bfloat16)
        own_real = demod[0].astype(jnp.float32)
        own_imag = demod[1].astype(jnp.float32)
        prod_real = []
        prod_imag = []
        for wheel in range(WHEELS):
            for order_at in range(ORDERS):
                partner = jnp.roll(demod, -orders[wheel, order_at], axis=1).astype(jnp.float32)
                prod_real.append(own_real * partner[0] + own_imag * partner[1])
                prod_imag.append(own_imag * partner[0] - own_real * partner[1])
        products = jnp.stack([jnp.stack(prod_real), jnp.stack(prod_imag)]).astype(jnp.bfloat16)
        grid = products.astype(jnp.float32).reshape(2, COMBOS, NCH, SUB, RADIX)
        first_real = jnp.einsum('ckab,aq->ckbq', grid[0], cos_sub) + jnp.einsum('ckab,aq->ckbq', grid[1], sin_sub)
        first_imag = jnp.einsum('ckab,aq->ckbq', grid[1], cos_sub) - jnp.einsum('ckab,aq->ckbq', grid[0], sin_sub)
        out_real, out_imag = finish_transform(first_real, first_imag, HOPS)
        spectra.append(jnp.stack([out_real, out_imag]).reshape(2, COMBOS, NCH, HOPS).astype(jnp.bfloat16))
        features.append(jnp.log1p(out_real * out_real + out_imag * out_imag).astype(jnp.bfloat16))
    spectrum = jnp.stack(spectra, axis=1)
    feature = jnp.stack(features)
    tiles = feature.reshape(SENSORS, COMBOS, devices_n, CH_DEV, RADIX, SUB)
    tiles = tiles.transpose(2, 0, 1, 4, 3, 5).reshape(devices_n, TILES_DEV, CH_DEV, SUB)
    owner_ids = owners[:, 0].reshape(devices_n, TILES_DEV)

    def score_block(block):
        block_tiles, block_owners = block
        return jnp.einsum('tkq,tqf->tkf', block_tiles.astype(jnp.float32), templates[block_owners].astype(jnp.float32)).astype(jnp.bfloat16)
    scores = lax.map(score_block, (tiles, owner_ids))
    targets = jnp.arange(devices_n, dtype=jnp.int32)
    one_hot = (owner_ids[:, :, None] == targets[None, None, :]).astype(jnp.int32)
    before = jnp.cumsum(one_hot, axis=1) - one_hot
    slot_ids = lax.optimization_barrier(jnp.sum(before * one_hot, axis=2)).astype(jnp.int32)
    sources = jnp.broadcast_to(targets[:, None], owner_ids.shape)
    detections = jnp.zeros((devices_n, devices_n, CAP, CH_DEV, FEAT), jnp.bfloat16)
    detections = detections.at[owner_ids, sources, slot_ids].set(scores)
    return (spectrum, detections)
```

```python
import functools
import math

import jax
import jax.numpy as jnp
from jax import lax
from jax.experimental import pallas as pl
from jax.experimental.pallas import tpu as pltpu
from jax.sharding import PartitionSpec as P

RADIX = 8
F32 = jnp.float32
BF16 = jnp.bfloat16


def channel_table(n_total, channel_ids):
    position = jnp.arange(n_total, dtype=jnp.int32)
    turns = position[None, :] * channel_ids[:, None] % n_total
    phase_angle = 2.0 * math.pi / n_total * turns.astype(F32)
    window = 0.5 - 0.5 * jnp.cos(2.0 * math.pi / n_total * position.astype(F32))
    weighted = math.sqrt(8.0 / (3.0 * n_total)) * window[None, :]
    both = jnp.concatenate(
        [weighted * jnp.cos(phase_angle), weighted * jnp.sin(phase_angle)], axis=0
    )
    return both.astype(BF16)


def sub_table(sub_total):
    index = jnp.arange(sub_total, dtype=jnp.int32)
    turns = index[:, None] * index[None, :] % sub_total
    phase_angle = 2.0 * math.pi / sub_total * turns.astype(F32)
    cos, sin = jnp.cos(phase_angle).astype(BF16), jnp.sin(phase_angle).astype(BF16)
    return jnp.concatenate(
        [jnp.concatenate([cos, -sin], axis=1), jnp.concatenate([sin, cos], axis=1)], axis=0
    )


def twist_table(sub_total, hops_total):
    index_b = jnp.arange(RADIX, dtype=jnp.int32)[:, None]
    index_p = jnp.arange(sub_total, dtype=jnp.int32)[None, :]
    angle = 2.0 * math.pi / hops_total * (index_b * index_p % hops_total).astype(F32)
    return jnp.concatenate([jnp.cos(angle), jnp.sin(angle)], axis=0) / math.sqrt(hops_total)


def dot_nt(a, b):
    return lax.dot_general(a, b, (((1,), (1,)), ((), ())), preferred_element_type=F32)


def four_point(y0, y1, y2, y3):
    s0 = (y0[0] + y2[0], y0[1] + y2[1])
    s1 = (y0[0] - y2[0], y0[1] - y2[1])
    s2 = (y1[0] + y3[0], y1[1] + y3[1])
    s3 = (y1[0] - y3[0], y1[1] - y3[1])
    return (
        (s0[0] + s2[0], s0[1] + s2[1]),
        (s1[0] + s3[1], s1[1] - s3[0]),
        (s0[0] - s2[0], s0[1] - s2[1]),
        (s1[0] - s3[1], s1[1] + s3[0]),
    )


def eight_point(x):
    even = four_point(x[0], x[2], x[4], x[6])
    odd = four_point(x[1], x[3], x[5], x[7])
    h = math.sqrt(0.5)
    o1, o2, o3 = odd[1], odd[2], odd[3]
    turned = (
        odd[0],
        ((o1[0] + o1[1]) * h, (o1[1] - o1[0]) * h),
        (o2[1], -o2[0]),
        ((o3[1] - o3[0]) * h, -(o3[0] + o3[1]) * h),
    )
    low = [(e[0] + t[0], e[1] + t[1]) for e, t in zip(even, turned)]
    high = [(e[0] - t[0], e[1] - t[1]) for e, t in zip(even, turned)]
    return low + high


def log_one_plus(x):
    return jnp.where(x < 2.0**-8, x * (1.0 - 0.5 * x), jnp.log(1.0 + x))


def spectra_kernel(
    orders_ref, owners_ref, places_ref, first_ref,
    frames_ref, coef_ref, table_ref, twist_ref, templates_ref,
    spectrum_ref, outgoing_ref,
    demod, product, section, feature,
    *, combos, per,
):
    sensor, combo = pl.program_id(0), pl.program_id(1)
    sub = table_ref.shape[0] // 2
    frame = frames_ref.shape[-1]
    wide = 2 * per

    @pl.when((sensor == 0) & (combo == 0))
    def _():
        outgoing_ref[...] = jnp.zeros_like(outgoing_ref)

    @pl.when(combo == 0)
    def _():
        channel = first_ref[0] + lax.broadcasted_iota(jnp.int32, (wide, sub), 0)
        last = lax.broadcasted_iota(jnp.int32, (2 * wide, sub), 1) == sub - 1
        for b in range(RADIX):
            total, ahead = None, None
            for quarter in range(4):
                hops = frames_ref[:, 0, (b + quarter) % RADIX].reshape(sub, frame)
                part = dot_nt(coef_ref[:, quarter * frame : (quarter + 1) * frame], hops)
                if b + quarter < RADIX:
                    total = part if total is None else total + part
                else:
                    ahead = part if ahead is None else ahead + part
            if ahead is not None:
                moved = pltpu.roll(ahead, sub - 1, 1)
                total = total + jnp.where(last, 0.0, moved)
            a_cos, a_sin = total[:wide], total[wide:]
            turn = channel % 4 * (b % 4) % 4
            swap = (turn == 1) | (turn == 3)
            real = jnp.where(swap, a_sin, a_cos)
            imag = jnp.where(swap, a_cos, a_sin)
            real = jnp.where((turn == 1) | (turn == 2), -real, real)
            imag = jnp.where((turn == 0) | (turn == 1), -imag, imag)
            demod[0, b] = real.astype(BF16)
            demod[1, b] = imag.astype(BF16)
        row = lax.broadcasted_iota(jnp.int32, (per, wide), 0)
        col = lax.broadcasted_iota(jnp.int32, (per, wide), 1)
        pick = jnp.concatenate(
            [(col == row + orders_ref[c]).astype(F32) for c in range(combos)], axis=0
        ).astype(BF16)
        for b in range(RADIX):
            part_real = jnp.dot(pick, demod[0, b], preferred_element_type=F32)
            part_imag = jnp.dot(pick, demod[1, b], preferred_element_type=F32)
            own_real = demod[0, b, :per].astype(F32)
            own_imag = demod[1, b, :per].astype(F32)
            for c in range(combos):
                pr = part_real[c * per : (c + 1) * per]
                pi = part_imag[c * per : (c + 1) * per]
                rows = slice(b * per, (b + 1) * per)
                product[c, rows, :sub] = (own_real * pr + own_imag * pi).astype(BF16)
                product[c, rows, sub:] = (own_imag * pr - own_real * pi).astype(BF16)

    section[...] = jnp.dot(product[combo], table_ref[...], preferred_element_type=F32)

    def rows_step(at, carry):
        start = pl.multiple_of(at * 16, 16)
        for lane in range(0, sub, 128):
            values = []
            for b in range(RADIX):
                here = pl.ds(b * per + start, 16)
                re = section[here, lane : lane + 128]
                im = section[here, sub + lane : sub + lane + 128]
                cos = twist_ref[b : b + 1, lane : lane + 128]
                sin = twist_ref[RADIX + b : RADIX + b + 1, lane : lane + 128]
                values.append((re * cos + im * sin, im * cos - re * sin))
            for d, (re, im) in enumerate(eight_point(values)):
                out = slice(d * sub + lane, d * sub + lane + 128)
                spectrum_ref[0, 0, 0, pl.ds(start, 16), out] = re.astype(BF16)
                spectrum_ref[1, 0, 0, pl.ds(start, 16), out] = im.astype(BF16)
                feature[d, pl.ds(start, 16), lane : lane + 128] = log_one_plus(
                    re * re + im * im
                ).astype(BF16)
        return carry

    lax.fori_loop(0, per // 16, rows_step, 0)

    first_tile = (sensor * combos + combo) * RADIX
    for d in range(RADIX):
        owner = owners_ref[first_tile + d]
        place = places_ref[first_tile + d]
        outgoing_ref[place] = jnp.dot(
            feature[d], templates_ref[owner], preferred_element_type=F32
        ).astype(BF16)


def shards(frames, orders, owners, templates):
    rows_count = lax.axis_size("row")
    cols_count = lax.axis_size("col")
    devices_n = rows_count * cols_count
    sensors, hop_dev, frame_len = frames.shape
    channels_n = 4 * frame_len
    hops_n = hop_dev * rows_count
    sub_n = hops_n // RADIX
    per = channels_n // devices_n
    combos = orders.shape[0] * orders.shape[1]
    feat_n = templates.shape[2]
    row_at = lax.axis_index("row")
    col_at = lax.axis_index("col")

    part = sub_n // devices_n
    mine = lax.dynamic_slice_in_dim(
        frames.reshape(sensors, hop_dev // RADIX, RADIX, frame_len), col_at * part, part, axis=1
    ).transpose(0, 2, 1, 3)
    hops = lax.all_gather(mine, ("row", "col"), axis=0)
    if part % 16:
        hops = hops.transpose(1, 2, 0, 3, 4).reshape(1, sensors, RADIX, sub_n, frame_len)
    gathered = lax.all_gather(templates, ("row", "col"), axis=0, tiled=True)

    first_channel = (row_at * cols_count + col_at) * per
    channel_ids = (first_channel + jnp.arange(2 * per, dtype=jnp.int32)) % channels_n
    coefficients = channel_table(channels_n, channel_ids)
    table = sub_table(sub_n)
    twist = twist_table(sub_n, hops_n)

    tiles_dev = sensors * combos * RADIX
    capacity = max(2, 2 * tiles_dev // devices_n)
    owner_ids = owners[:, 0]
    index = jnp.arange(tiles_dev, dtype=jnp.int32)
    earlier = (owner_ids[None, :] == owner_ids[:, None]) & (index[None, :] < index[:, None])
    places = owner_ids * capacity + jnp.sum(earlier.astype(jnp.int32), axis=1)

    whole = lambda shape: pl.BlockSpec(
        shape, lambda s, c, *_: (0,) * len(shape), pipeline_mode=pl.Buffered(1)
    )
    blocks = hops.shape[0]
    flops = 2 * sensors * hops_n * channels_n * 4 * per + 2 * sensors * combos * RADIX * per * 4 * sub_n * sub_n
    spectrum, outgoing = pl.pallas_call(
        functools.partial(spectra_kernel, combos=combos, per=per),
        grid_spec=pltpu.PrefetchScalarGridSpec(
            num_scalar_prefetch=4,
            grid=(sensors, combos),
            in_specs=[
                pl.BlockSpec(
                    (blocks, 1, RADIX, hops.shape[3], frame_len),
                    lambda s, c, *_: (0, s, 0, 0, 0),
                ),
                whole(coefficients.shape),
                whole(table.shape),
                whole(twist.shape),
                whole(gathered.shape),
            ],
            out_specs=[
                pl.BlockSpec((2, 1, 1, per, hops_n), lambda s, c, *_: (0, s, c, 0, 0)),
                whole((devices_n * capacity, per, feat_n)),
            ],
            scratch_shapes=[
                pltpu.VMEM((2, RADIX, 2 * per, sub_n), BF16),
                pltpu.VMEM((combos, RADIX * per, 2 * sub_n), BF16),
                pltpu.VMEM((RADIX * per, 2 * sub_n), F32),
                pltpu.VMEM((RADIX, per, sub_n), BF16),
            ],
        ),
        out_shape=[
            jax.ShapeDtypeStruct((2, sensors, combos, per, hops_n), BF16),
            jax.ShapeDtypeStruct((devices_n * capacity, per, feat_n), BF16),
        ],
        compiler_params=pltpu.CompilerParams(
            vmem_limit_bytes=52 * 2**20,
            dimension_semantics=("arbitrary", "arbitrary"),
        ),
        cost_estimate=pl.CostEstimate(
            flops=flops, bytes_accessed=64 * 2**20, transcendentals=sensors * combos * per * hops_n
        ),
    )(
        orders.reshape(-1), owner_ids, places, first_channel.reshape(1),
        hops, coefficients, table, twist, gathered,
    )
    outgoing = outgoing.reshape(devices_n, capacity, per, feat_n)
    found = lax.all_to_all(outgoing, ("row", "col"), split_axis=0, concat_axis=0, tiled=True)
    return (spectrum, found[None])


def solution(mesh):
    in_specs = (P(None, "row", None), P(), P(("row", "col"), None), P(("row", "col"), None, None))
    out_specs = (
        P(None, None, None, ("row", "col"), None),
        P(("row", "col"), None, None, None, None),
    )
    return jax.shard_map(shards, mesh=mesh, in_specs=in_specs, out_specs=out_specs, check_vma=False)
```

```python
import functools
import math

import jax
import jax.numpy as jnp
from jax import lax
from jax.experimental import pallas as pl
from jax.experimental.pallas import tpu as pltpu
from jax.sharding import PartitionSpec as P

RADIX = 8
F32 = jnp.float32
BF16 = jnp.bfloat16


def channel_table(n_total, channel_ids):
    position = jnp.arange(n_total, dtype=jnp.int32)
    turns = position[None, :] * channel_ids[:, None] % n_total
    phase_angle = 2.0 * math.pi / n_total * turns.astype(F32)
    window = 0.5 - 0.5 * jnp.cos(2.0 * math.pi / n_total * position.astype(F32))
    weighted = math.sqrt(8.0 / (3.0 * n_total)) * window[None, :]
    both = jnp.concatenate(
        [weighted * jnp.cos(phase_angle), weighted * jnp.sin(phase_angle)], axis=0
    )
    return both.astype(BF16)


def sub_table(sub_total):
    index = jnp.arange(sub_total, dtype=jnp.int32)
    turns = index[:, None] * index[None, :] % sub_total
    phase_angle = 2.0 * math.pi / sub_total * turns.astype(F32)
    cos, sin = jnp.cos(phase_angle).astype(BF16), jnp.sin(phase_angle).astype(BF16)
    return jnp.concatenate(
        [jnp.concatenate([cos, -sin], axis=1), jnp.concatenate([sin, cos], axis=1)], axis=0
    )


def twist_table(sub_total, hops_total):
    index_b = jnp.arange(RADIX, dtype=jnp.int32)[:, None]
    index_p = jnp.arange(sub_total, dtype=jnp.int32)[None, :]
    angle = 2.0 * math.pi / hops_total * (index_b * index_p % hops_total).astype(F32)
    return jnp.concatenate([jnp.cos(angle), jnp.sin(angle)], axis=0) / math.sqrt(hops_total)


def dot_nt(a, b):
    return lax.dot_general(a, b, (((1,), (1,)), ((), ())), preferred_element_type=F32)


def four_point(y0, y1, y2, y3):
    s0 = (y0[0] + y2[0], y0[1] + y2[1])
    s1 = (y0[0] - y2[0], y0[1] - y2[1])
    s2 = (y1[0] + y3[0], y1[1] + y3[1])
    s3 = (y1[0] - y3[0], y1[1] - y3[1])
    return (
        (s0[0] + s2[0], s0[1] + s2[1]),
        (s1[0] + s3[1], s1[1] - s3[0]),
        (s0[0] - s2[0], s0[1] - s2[1]),
        (s1[0] - s3[1], s1[1] + s3[0]),
    )


def eight_point(x):
    even = four_point(x[0], x[2], x[4], x[6])
    odd = four_point(x[1], x[3], x[5], x[7])
    h = math.sqrt(0.5)
    o1, o2, o3 = odd[1], odd[2], odd[3]
    turned = (
        odd[0],
        ((o1[0] + o1[1]) * h, (o1[1] - o1[0]) * h),
        (o2[1], -o2[0]),
        ((o3[1] - o3[0]) * h, -(o3[0] + o3[1]) * h),
    )
    low = [(e[0] + t[0], e[1] + t[1]) for e, t in zip(even, turned)]
    high = [(e[0] - t[0], e[1] - t[1]) for e, t in zip(even, turned)]
    return low + high


def log_one_plus(x):
    return jnp.where(x < 2.0**-8, x * (1.0 - 0.5 * x), jnp.log(1.0 + x))


def spectra_kernel(
    orders_ref, owners_ref, places_ref, first_ref,
    frames_ref, coef_ref, table_ref, twist_ref, templates_ref,
    *rest, combos, per, base,
):
    spectrum_ref, outgoing_ref, demod, product, section, feature = rest[-6:]
    sensor, combo = pl.program_id(0), pl.program_id(1)
    sub = table_ref.shape[0] // 2
    frame = frames_ref.shape[-1]
    wide = 2 * per

    @pl.when((sensor == 0) & (combo == 0))
    def _():
        outgoing_ref[...] = rest[1][...] if base else jnp.zeros_like(outgoing_ref)

    @pl.when(combo == 0)
    def _():
        channel = first_ref[0] + lax.broadcasted_iota(jnp.int32, (wide, sub), 0)
        last = lax.broadcasted_iota(jnp.int32, (2 * wide, sub), 1) == sub - 1
        for b in range(RADIX):
            total, ahead = None, None
            for quarter in range(4):
                hops = frames_ref[:, 0, (b + quarter) % RADIX].reshape(sub, frame)
                part = dot_nt(coef_ref[:, quarter * frame : (quarter + 1) * frame], hops)
                if b + quarter < RADIX:
                    total = part if total is None else total + part
                else:
                    ahead = part if ahead is None else ahead + part
            if ahead is not None:
                moved = pltpu.roll(ahead, sub - 1, 1)
                total = total + jnp.where(last, 0.0, moved)
            a_cos, a_sin = total[:wide], total[wide:]
            turn = channel % 4 * (b % 4) % 4
            swap = (turn == 1) | (turn == 3)
            real = jnp.where(swap, a_sin, a_cos)
            imag = jnp.where(swap, a_cos, a_sin)
            real = jnp.where((turn == 1) | (turn == 2), -real, real)
            imag = jnp.where((turn == 0) | (turn == 1), -imag, imag)
            demod[0, b] = real.astype(BF16)
            demod[1, b] = imag.astype(BF16)
        row = lax.broadcasted_iota(jnp.int32, (per, wide), 0)
        col = lax.broadcasted_iota(jnp.int32, (per, wide), 1)
        pick = jnp.concatenate(
            [(col == row + orders_ref[c]).astype(F32) for c in range(combos)], axis=0
        ).astype(BF16)
        for b in range(RADIX):
            part_real = jnp.dot(pick, demod[0, b], preferred_element_type=F32)
            part_imag = jnp.dot(pick, demod[1, b], preferred_element_type=F32)
            own_real = demod[0, b, :per].astype(F32)
            own_imag = demod[1, b, :per].astype(F32)
            for c in range(combos):
                pr = part_real[c * per : (c + 1) * per]
                pi = part_imag[c * per : (c + 1) * per]
                rows = slice(b * per, (b + 1) * per)
                product[c, rows, :sub] = (own_real * pr + own_imag * pi).astype(BF16)
                product[c, rows, sub:] = (own_imag * pr - own_real * pi).astype(BF16)

    section[...] = jnp.dot(product[combo], table_ref[...], preferred_element_type=F32)

    def rows_step(at, carry):
        start = pl.multiple_of(at * 16, 16)
        for lane in range(0, sub, 128):
            values = []
            for b in range(RADIX):
                here = pl.ds(b * per + start, 16)
                re = section[here, lane : lane + 128]
                im = section[here, sub + lane : sub + lane + 128]
                cos = twist_ref[b : b + 1, lane : lane + 128]
                sin = twist_ref[RADIX + b : RADIX + b + 1, lane : lane + 128]
                values.append((re * cos + im * sin, im * cos - re * sin))
            for d, (re, im) in enumerate(eight_point(values)):
                out = slice(d * sub + lane, d * sub + lane + 128)
                spectrum_ref[0, 0, 0, pl.ds(start, 16), out] = re.astype(BF16)
                spectrum_ref[1, 0, 0, pl.ds(start, 16), out] = im.astype(BF16)
                feature[d, pl.ds(start, 16), lane : lane + 128] = log_one_plus(
                    re * re + im * im
                ).astype(BF16)
        return carry

    lax.fori_loop(0, per // 16, rows_step, 0)

    first_tile = ((base + sensor) * combos + combo) * RADIX
    for d in range(RADIX):
        owner = owners_ref[first_tile + d]
        place = places_ref[first_tile + d]
        outgoing_ref[place] = jnp.dot(
            feature[d], templates_ref[owner], preferred_element_type=F32
        ).astype(BF16)


def shards(frames, orders, owners, templates):
    rows_count = lax.axis_size("row")
    cols_count = lax.axis_size("col")
    devices_n = rows_count * cols_count
    sensors, hop_dev, frame_len = frames.shape
    channels_n = 4 * frame_len
    hops_n = hop_dev * rows_count
    sub_n = hops_n // RADIX
    per = channels_n // devices_n
    combos = orders.shape[0] * orders.shape[1]
    feat_n = templates.shape[2]
    row_at = lax.axis_index("row")
    col_at = lax.axis_index("col")

    part = sub_n // devices_n
    mine = lax.dynamic_slice_in_dim(
        frames.reshape(sensors, hop_dev // RADIX, RADIX, frame_len), col_at * part, part, axis=1
    ).transpose(0, 2, 1, 3)
    half = sensors // 2
    parts = []
    for at in (0, half):
        hops = lax.all_gather(mine[at : at + half], ("row", "col"), axis=0)
        if part % 16:
            hops = hops.transpose(1, 2, 0, 3, 4).reshape(1, half, RADIX, sub_n, frame_len)
        parts.append(hops)
    gathered = lax.all_gather(templates, ("row", "col"), axis=0, tiled=True)

    first_channel = (row_at * cols_count + col_at) * per
    channel_ids = (first_channel + jnp.arange(2 * per, dtype=jnp.int32)) % channels_n
    coefficients = channel_table(channels_n, channel_ids)
    table = sub_table(sub_n)
    twist = twist_table(sub_n, hops_n)

    tiles_dev = sensors * combos * RADIX
    capacity = max(2, 2 * tiles_dev // devices_n)
    owner_ids = owners[:, 0]
    index = jnp.arange(tiles_dev, dtype=jnp.int32)
    earlier = (owner_ids[None, :] == owner_ids[:, None]) & (index[None, :] < index[:, None])
    places = owner_ids * capacity + jnp.sum(earlier.astype(jnp.int32), axis=1)

    whole = lambda shape: pl.BlockSpec(
        shape, lambda s, c, *_: (0,) * len(shape), pipeline_mode=pl.Buffered(1)
    )
    prior = ()
    for base, hops in zip((0, half), parts):
        blocks = hops.shape[0]
        flops = 2 * half * hops_n * channels_n * 4 * per + 2 * half * combos * RADIX * per * 4 * sub_n * sub_n
        prior = pl.pallas_call(
            functools.partial(spectra_kernel, combos=combos, per=per, base=base),
            grid_spec=pltpu.PrefetchScalarGridSpec(
                num_scalar_prefetch=4,
                grid=(half, combos),
                in_specs=[
                    pl.BlockSpec(
                        (blocks, 1, RADIX, hops.shape[3], frame_len),
                        lambda s, c, *_: (0, s, 0, 0, 0),
                    ),
                    whole(coefficients.shape),
                    whole(table.shape),
                    whole(twist.shape),
                    whole(gathered.shape),
                ] + ([pl.BlockSpec(memory_space=pl.ANY), whole(prior[1].shape)] if base else []),
                out_specs=[
                    pl.BlockSpec((2, 1, 1, per, hops_n), lambda s, c, *_: (0, base + s, c, 0, 0)),
                    whole((devices_n * capacity, per, feat_n)),
                ],
                scratch_shapes=[
                    pltpu.VMEM((2, RADIX, 2 * per, sub_n), BF16),
                    pltpu.VMEM((combos, RADIX * per, 2 * sub_n), BF16),
                    pltpu.VMEM((RADIX * per, 2 * sub_n), F32),
                    pltpu.VMEM((RADIX, per, sub_n), BF16),
                ],
            ),
            out_shape=[
                jax.ShapeDtypeStruct((2, sensors, combos, per, hops_n), BF16),
                jax.ShapeDtypeStruct((devices_n * capacity, per, feat_n), BF16),
            ],
            input_output_aliases={9: 0} if base else {},
            compiler_params=pltpu.CompilerParams(
                vmem_limit_bytes=52 * 2**20,
                dimension_semantics=("arbitrary", "arbitrary"),
            ),
            cost_estimate=pl.CostEstimate(
                flops=flops, bytes_accessed=32 * 2**20, transcendentals=half * combos * per * hops_n
            ),
        )(
            orders.reshape(-1), owner_ids, places, first_channel.reshape(1),
            hops, coefficients, table, twist, gathered, *prior,
        )
    spectrum, outgoing = prior
    outgoing = outgoing.reshape(devices_n, capacity, per, feat_n)
    found = lax.all_to_all(outgoing, ("row", "col"), split_axis=0, concat_axis=0, tiled=True)
    return (spectrum, found[None])


def solution(mesh):
    in_specs = (P(None, "row", None), P(), P(("row", "col"), None), P(("row", "col"), None, None))
    out_specs = (
        P(None, None, None, ("row", "col"), None),
        P(("row", "col"), None, None, None, None),
    )
    return jax.shard_map(shards, mesh=mesh, in_specs=in_specs, out_specs=out_specs, check_vma=False)
```
